32 devices in a mesh: groups: 2 (over y), train: 4 (over z), layer: 4 (over x, core).
Axes of the slice: x: 2, y: 2, z: 4, core: 2. Of those that a mesh axis runs over, the one named last changes fastest.
Arguments:
- query_grads: bfloat16 [1024, 4, 4096], P('train', 'layer'), may hold values from -6 to 6
- train_grads: bfloat16 [8192, 4, 4096], P(('groups', 'train'), 'layer'), parts along dimension 0, may hold values from -0.046875 to 0.046875
- left_inverse: float32 [4, 64, 64], P('layer')
- right_inverse: float32 [4, 64, 64], P('layer')
- valid_rows: int32 [8], P(('groups', 'train')), parts along dimension 0, may hold values from 256 to 1024, as said below
- query_order: int32 [1024], replicated, may hold values from 0 to 1023, each once
Outputs:
- scores: float32 [1024, 8192], P('layer', ('groups', 'train')), parts along dimension 1
The draws below stay inside these ranges and needn't reach their ends.
There are 2 independent parts, one for each index of `groups`. The reference program is written for one: setup_inputs(seed, part) draws one part's arguments, and reference() takes and returns one part's arrays. A program takes and returns all parts, laid end to end along the dimension named above; an argument that names none is the same for every part. Nothing has to cross between parts.
Inputs may be any that keep to these rules, and one draw needn't show every extreme that they name: `query_order`: a permutation: every query appears once. `valid_rows`: in every draw one shard has all 1024 slots live and another has 256.
All inputs are finite; a program needn't handle non-finite values.
Results may differ from the reference program's by a relative error of at most 0.0029.
Values may be sent and summed in bfloat16 or wider, within the bound.
A program may use at most 64 MiB of HBM per device.

```python
import math
import jax
import jax.numpy as jnp
from jax import lax

KIN = 64
KOUT = 64
P_SIZE = 4096
Q = 1024
TR_DEV = 1024
L = 4
TRAIN = 4096
N_TRAIN = 4


def inverse_factor(key, layer_count, order, off_scale, row_spread):
    key_diag, key_off, key_rows = jax.random.split(key, 3)
    identity = jnp.eye(order, dtype=jnp.float32)
    diagonal = jnp.exp(jax.random.uniform(key_diag, (layer_count, order), jnp.float32, math.log(0.5), math.log(2.0)))
    spread = jax.random.normal(key_off, (layer_count, order, order), jnp.float32) * off_scale
    row_scale = jnp.exp(jax.random.uniform(key_rows, (layer_count, order, 1), jnp.float32, 0.0, math.log(row_spread)))
    matrix = identity[None, :, :] * diagonal[:, :, None] + spread * (1.0 - identity[None, :, :])
    return (matrix * row_scale).astype(jnp.float32)


def draw_left_inverse(key, part):
    key = jax.random.fold_in(key, 11)
    return inverse_factor(key, L, KIN, 0.06, 1.0)


def draw_right_inverse(key, part):
    key = jax.random.fold_in(key, 17)
    return inverse_factor(key, L, KOUT, 0.06, 1.0)


def draw_valid_rows(key, part):
    key = jax.random.fold_in(key, 23)
    key_counts, key_full, key_low = jax.random.split(key, 3)
    counts = jax.random.randint(key_counts, (N_TRAIN,), TR_DEV // 4, TR_DEV + 1, dtype=jnp.int32)
    full_shard = jax.random.randint(key_full, (), 0, N_TRAIN, dtype=jnp.int32)
    low_shard = (full_shard + 1 + jax.random.randint(key_low, (), 0, N_TRAIN - 1, dtype=jnp.int32)) % N_TRAIN
    shard_ids = jnp.arange(N_TRAIN, dtype=jnp.int32)
    counts = jnp.where(shard_ids == full_shard, TR_DEV, counts)
    counts = jnp.where(shard_ids == low_shard, TR_DEV // 4, counts)
    return counts.astype(jnp.int32)


def steps_of(rng, extent, cuts, smallest, high):
    def one(position, blocks):
        heights = jax.random.uniform(jax.random.fold_in(jax.random.fold_in(rng, 6), position), (blocks,), jnp.float32, smallest / len(cuts), high / len(cuts))
        return jnp.repeat(jnp.exp(heights), extent[position] // blocks).reshape((-1,) + (1,) * (len(extent) - position - 1))

    level = one(*cuts[0])
    for cut in cuts[1:]:
        level = level * one(*cut)
    return level


def noise(stream_key, dims, scale, bound, cuts=(), kind=jnp.bfloat16):
    gain = steps_of(stream_key, dims, cuts, -0.22, 0.18) if cuts else 1.0
    drawn = jax.random.normal(stream_key, dims, jnp.float32) * scale * gain
    return jnp.minimum(jnp.maximum(drawn, -bound), bound).astype(kind)


def setup_inputs(seed: int = 0, part: int = 0) -> dict:
    arg_keys = jax.random.split(jax.random.key(seed), 7)
    part_keys = jax.random.split(jax.random.fold_in(arg_keys[6], part), 7)
    query_grads = noise(arg_keys[0], (Q, L, P_SIZE), 1.0, 6.0, ((0, 4), (1, 4)))
    train_grads = noise(part_keys[1], (TRAIN, L, P_SIZE), (L * KIN * KOUT) ** -0.5, 0.046875, ((0, 4), (1, 4)))
    left_inverse = draw_left_inverse(jax.random.fold_in(arg_keys[6], 71), part)
    right_inverse = draw_right_inverse(jax.random.fold_in(arg_keys[6], 71), part)
    valid_rows = draw_valid_rows(jax.random.fold_in(jax.random.fold_in(arg_keys[6], part), 71), part)
    query_order = jax.random.permutation(arg_keys[5], Q).astype(jnp.int32)
    return {"query_grads": query_grads, "train_grads": train_grads, "left_inverse": left_inverse, "right_inverse": right_inverse, "valid_rows": valid_rows, "query_order": query_order}


def precondition(gradients, left_factor, right_factor):
    row_count = gradients.shape[0]
    layer_count = left_factor.shape[0]
    order_in = left_factor.shape[-1]
    order_out = right_factor.shape[-1]
    matrix = gradients.astype(jnp.float32).reshape(row_count, layer_count, order_in, order_out)
    matrix = jnp.einsum("lab,rlbc->rlac", left_factor, matrix, precision=lax.Precision.HIGHEST)
    matrix = jnp.einsum("rlac,lcd->rlad", matrix, right_factor, precision=lax.Precision.HIGHEST)
    return matrix.reshape(row_count, layer_count, order_in * order_out).astype(jnp.bfloat16)


def reference(query_grads, train_grads, left_inverse, right_inverse, valid_rows, query_order):
    conditioned = precondition(query_grads, left_inverse, right_inverse)
    train_count = train_grads.shape[0]
    layer_count = left_inverse.shape[0]

    def layer_step(totals, layer_index):
        query_slab = lax.dynamic_index_in_dim(conditioned, layer_index, 1, keepdims=False).astype(jnp.float32)
        train_slab = lax.dynamic_index_in_dim(train_grads, layer_index, 1, keepdims=False).astype(jnp.float32)
        product = lax.dot_general(query_slab, train_slab, (((1,), (1,)), ((), ())))
        return totals + product, 0

    start_totals = jnp.zeros((query_grads.shape[0], train_count), jnp.float32)
    raw_scores, unused = lax.scan(layer_step, start_totals, jnp.arange(layer_count, dtype=jnp.int32))
    slot_ids = jnp.arange(train_count, dtype=jnp.int32)
    shard_ids = slot_ids // TR_DEV
    live_mask = (slot_ids % TR_DEV) < jnp.take(valid_rows, shard_ids)
    ordered = jnp.take(raw_scores, query_order, axis=0)
    return jnp.where(live_mask[None, :], ordered, jnp.zeros_like(ordered))
```

```python
import jax
import jax.numpy as jnp
from jax import lax
from jax.sharding import PartitionSpec as P


def precondition(gradients, left_factor, right_factor):
    row_count = gradients.shape[0]
    layer_count = left_factor.shape[0]
    order_in = left_factor.shape[-1]
    order_out = right_factor.shape[-1]
    matrix = gradients.astype(jnp.float32).reshape(row_count, layer_count, order_in, order_out)
    matrix = jnp.einsum("lab,rlbc->rlac", left_factor, matrix, precision=lax.Precision.HIGHEST)
    matrix = jnp.einsum("rlac,lcd->rlad", matrix, right_factor, precision=lax.Precision.HIGHEST)
    return matrix.reshape(row_count, layer_count, order_in * order_out).astype(jnp.bfloat16)


def summed_over_layers(partial):
    size = lax.axis_size("layer")
    me = lax.axis_index("layer")
    columns = partial.shape[-1]
    blocks = partial.reshape(size, -1, columns)
    step = 1
    while step < size:
        count = size // step
        halves = blocks.reshape(count // 2, 2, -1, columns)
        bit = (me // step) % 2
        kept = lax.dynamic_index_in_dim(halves, bit, 1, keepdims=False)
        given = lax.dynamic_index_in_dim(halves, 1 - bit, 1, keepdims=False)
        if step > 1:
            given = given.astype(jnp.bfloat16)
        route = [(i, i ^ step) for i in range(size)]
        taken = lax.ppermute(given, "layer", route)
        blocks = kept + taken.astype(jnp.float32)
        step *= 2
    return blocks.reshape(-1, columns)


def body(query_grads, train_grads, left_inverse, right_inverse, valid_rows, query_order):
    groups = lax.axis_size("groups")
    share = query_grads.shape[0] // groups
    own = lax.dynamic_slice_in_dim(query_grads, lax.axis_index("groups") * share, share, 0)
    conditioned = precondition(own, left_inverse, right_inverse).reshape(share, -1)
    conditioned = lax.all_gather(conditioned, ("train", "groups"), axis=0, tiled=True)
    train_flat = train_grads.reshape(train_grads.shape[0], -1)
    product = lax.dot_general(
        conditioned, train_flat, (((1,), (1,)), ((), ())), preferred_element_type=jnp.float32
    )
    live = jnp.arange(train_flat.shape[0], dtype=jnp.int32) < valid_rows[0]
    product = jnp.where(live[None, :], product, 0.0)
    ordered = jnp.take(product, query_order, axis=0)
    return summed_over_layers(ordered)


def solution(mesh):
    return jax.shard_map(
        body,
        mesh=mesh,
        in_specs=(
            P("train", "layer", None),
            P(("groups", "train"), "layer", None),
            P("layer", None, None),
            P("layer", None, None),
            P(("groups", "train")),
            P(),
        ),
        out_specs=P("layer", ("groups", "train")),
        check_vma=False,
    )
```

```python
import functools

import jax
import jax.numpy as jnp
from jax import lax
from jax.experimental import pallas as pl
from jax.experimental.pallas import tpu as pltpu
from jax.sharding import PartitionSpec as P


def precondition(gradients, left_factor, right_factor):
    row_count = gradients.shape[0]
    layer_count = left_factor.shape[0]
    order_in = left_factor.shape[-1]
    order_out = right_factor.shape[-1]
    matrix = gradients.astype(jnp.float32).reshape(row_count, layer_count, order_in, order_out)
    matrix = jnp.einsum("lab,rlbc->rlac", left_factor, matrix, precision=lax.Precision.HIGHEST)
    matrix = jnp.einsum("rlac,lcd->rlad", matrix, right_factor, precision=lax.Precision.HIGHEST)
    return matrix.reshape(row_count, layer_count, order_in * order_out).astype(jnp.bfloat16)


def summed_over_layers(partial):
    size = lax.axis_size("layer")
    me = lax.axis_index("layer")
    columns = partial.shape[-1]
    blocks = partial.reshape(size, -1, columns)
    step = 1
    while step < size:
        count = size // step
        halves = blocks.reshape(count // 2, 2, -1, columns)
        bit = (me // step) % 2
        kept = lax.dynamic_index_in_dim(halves, bit, 1, keepdims=False)
        given = lax.dynamic_index_in_dim(halves, 1 - bit, 1, keepdims=False)
        if step > 1:
            given = given.astype(jnp.bfloat16)
        route = [(i, i ^ step) for i in range(size)]
        taken = lax.ppermute(given, "layer", route)
        blocks = kept + taken.astype(jnp.float32)
        step *= 2
    return blocks.reshape(-1, columns)


def gather_and_score(cycle, chunks, own_ref, train_ref, product_ref, gathered, train, z_send, z_recv, y_send, y_recv, train_sem):
    position = lax.axis_index("train")
    group = lax.axis_index("groups")
    block = own_ref.shape[0]
    share = block // 2
    rows = share // chunks
    width = train.shape[0] // chunks
    load = pltpu.make_async_copy(train_ref, train, train_sem)
    load.start()

    has = (position > 0, position < cycle - 1)
    neighbour = ((position + cycle - 1) % cycle, (position + 1) % cycle)
    other = 1 - group
    barrier = pltpu.get_barrier_semaphore()
    for side in range(2):

        @pl.when(has[side])
        def _(side=side):
            pl.semaphore_signal(barrier, inc=1, device_id={"train": neighbour[side]}, device_id_type=pl.DeviceIdType.MESH)

    pl.semaphore_signal(barrier, inc=1, device_id={"groups": other}, device_id_type=pl.DeviceIdType.MESH)
    pl.semaphore_wait(barrier, 1 + has[0].astype(jnp.int32) + has[1].astype(jnp.int32))

    def place(index, half, chunk):
        return pl.ds(pl.multiple_of(index * block + half * share + chunk * rows, rows), rows)

    def along_z(side, index, distance, chunk, source):
        return pltpu.make_async_remote_copy(
            src_ref=source,
            dst_ref=gathered.at[place(index, group, chunk)],
            send_sem=z_send.at[side, distance, chunk],
            recv_sem=z_recv.at[side, distance, chunk],
            device_id={"train": neighbour[side]},
            device_id_type=pl.DeviceIdType.MESH,
        )

    def along_y(side, index, half, distance, chunk):
        return pltpu.make_async_remote_copy(
            src_ref=gathered.at[place(index, half, chunk)],
            dst_ref=gathered.at[place(index, half, chunk)],
            send_sem=y_send.at[side, distance, chunk],
            recv_sem=y_recv.at[side, distance, chunk],
            device_id={"groups": other},
            device_id_type=pl.DeviceIdType.MESH,
        )

    def own(chunk):
        return own_ref.at[pl.ds(pl.multiple_of(group * share + chunk * rows, rows), rows)]

    def first(chunk, _):
        for side in range(2):

            @pl.when(has[side])
            def _(side=side):
                along_z(side, position, 0, chunk, own(chunk)).start()

        return 0

    lax.fori_loop(0, chunks, first, 0)
    load.wait()

    def score(source, index, chunk):
        columns = pl.ds(pl.multiple_of(chunk * width, width), width)
        product_ref[pl.ds(pl.multiple_of(index * block, block), block), columns] = lax.dot_general(
            source, train[columns, :], (((1,), (1,)), ((), ())), preferred_element_type=jnp.float32
        )

    def turn(step, _):
        def slot(chunk, _):
            for side in range(2):
                index = position - 1 - step if side == 1 else position + 1 + step
                arrives = index >= 0 if side == 1 else index < cycle

                @pl.when(arrives)
                def _(side=side, index=index):
                    here = gathered.at[place(index, group, chunk)]
                    along_z(side, index, step, chunk, here).wait_recv()

                    @pl.when(has[side])
                    def _():
                        along_z(side, index, step + 1, chunk, here).start()

                    along_y(side, index, group, step, chunk).start()

            for side in range(2):
                index = position - step if side == 1 else position + step
                arrived = index >= 0 if side == 1 else index < cycle

                @pl.when((step > 0) & arrived)
                def _(side=side, index=index):
                    @pl.when(chunk == 0)
                    def _():
                        def landed(piece, _):
                            along_y(side, index, other, step - 1, piece).wait_recv()
                            return 0

                        lax.fori_loop(0, chunks, landed, 0)

                    score(gathered[pl.ds(pl.multiple_of(index * block, block), block), :], index, chunk)

            @pl.when(step == 0)
            def _():
                score(own_ref[...], position, chunk)

            return 0

        return lax.fori_loop(0, chunks, slot, 0)

    lax.fori_loop(0, cycle, turn, 0)

    def sent(step, _):
        def piece(chunk, _):
            for side in range(2):
                index = position - step if side == 1 else position + step
                held = index >= 0 if side == 1 else index < cycle

                @pl.when(held & has[side])
                def _(side=side, index=index):
                    along_z(side, position, step, chunk, own(chunk)).wait_send()

                came = index - 1 >= 0 if side == 1 else index + 1 < cycle

                @pl.when(came)
                def _(side=side):
                    along_y(side, position, group, step, chunk).wait_send()

            return 0

        return lax.fori_loop(0, chunks, piece, 0)

    lax.fori_loop(0, cycle, sent, 0)


def scores_of(conditioned, train_flat):
    cycle = lax.axis_size("train")
    block, depth = conditioned.shape
    slots = train_flat.shape[0]
    chunks = max(1, min(4, block // 2 // 16))
    return pl.pallas_call(
        functools.partial(gather_and_score, cycle, chunks),
        out_shape=jax.ShapeDtypeStruct((cycle * block, slots), jnp.float32),
        in_specs=[pl.BlockSpec(memory_space=pltpu.VMEM), pl.BlockSpec(memory_space=pl.ANY)],
        out_specs=pl.BlockSpec(memory_space=pltpu.VMEM),
        scratch_shapes=[
            pltpu.VMEM((cycle * block, depth), jnp.bfloat16),
            pltpu.VMEM((slots, depth), jnp.bfloat16),
            pltpu.SemaphoreType.DMA((2, cycle, chunks)),
            pltpu.SemaphoreType.DMA((2, cycle, chunks)),
            pltpu.SemaphoreType.DMA((2, cycle, chunks)),
            pltpu.SemaphoreType.DMA((2, cycle, chunks)),
            pltpu.SemaphoreType.DMA,
        ],
        compiler_params=pltpu.CompilerParams(
            collective_id=0, has_side_effects=True, vmem_limit_bytes=48 * 1024 * 1024
        ),
        cost_estimate=pl.CostEstimate(flops=2 * cycle * block * slots * depth, bytes_accessed=2 * slots * depth, transcendentals=0),
    )(conditioned, train_flat)


def body(query_grads, train_grads, left_inverse, right_inverse, valid_rows, query_order):
    conditioned = precondition(query_grads, left_inverse, right_inverse).reshape(query_grads.shape[0], -1)
    product = scores_of(conditioned, train_grads.reshape(train_grads.shape[0], -1))
    ordered = jnp.take(product, query_order, axis=0)
    scores = summed_over_layers(ordered)
    live = jnp.arange(scores.shape[1], dtype=jnp.int32) < valid_rows[0]
    return jnp.where(live[None, :], scores, 0.0)


def solution(mesh):
    return jax.shard_map(
        body,
        mesh=mesh,
        in_specs=(
            P("train", "layer", None),
            P(("groups", "train"), "layer", None),
            P("layer", None, None),
            P("layer", None, None),
            P(("groups", "train")),
            P(),
        ),
        out_specs=P("layer", ("groups", "train")),
        check_vma=False,
    )
```

```python
import functools

import jax
import jax.numpy as jnp
from jax import lax
from jax.experimental import pallas as pl
from jax.experimental.pallas import tpu as pltpu
from jax.sharding import PartitionSpec as P


def precondition(gradients, left_factor, right_factor):
    row_count = gradients.shape[0]
    layer_count = left_factor.shape[0]
    order_in = left_factor.shape[-1]
    order_out = right_factor.shape[-1]
    matrix = gradients.astype(jnp.float32).reshape(row_count, layer_count, order_in, order_out)
    matrix = jnp.einsum("lab,rlbc->rlac", left_factor, matrix, precision=lax.Precision.HIGHEST)
    matrix = jnp.einsum("rlac,lcd->rlad", matrix, right_factor, precision=lax.Precision.HIGHEST)
    return matrix.reshape(row_count, layer_count, order_in * order_out).astype(jnp.bfloat16)


MESH = pl.DeviceIdType.MESH


def gather_and_score(cycle, chunks, stages, own_ref, train_ref, order_ref, out_ref, gathered, train, give, taken, total, x_out, x_in, handed,
                     z_send, z_recv, y_send, y_recv, c_send, c_recv, x_send, x_recv, local_sem, last_sem):
    position = lax.axis_index("train")
    group = lax.axis_index("groups")
    layer = lax.axis_index("layer")
    core = layer % 2
    block = own_ref.shape[0]
    share = block // 2
    rows = share // chunks
    parts = chunks // 2
    width = train.shape[0] // chunks
    half = parts * width
    load = pltpu.make_async_copy(train_ref, train, local_sem.at[0])
    load.start()

    def block_of(index):
        return pl.ds(pl.multiple_of(index * block, block), block)

    move = pltpu.make_async_copy(own_ref, gathered.at[block_of(position)], local_sem.at[1])
    move.start()

    has = (position > 0, position < cycle - 1)
    neighbour = ((position + cycle - 1) % cycle, (position + 1) % cycle)
    other = 1 - group
    sibling = layer + 1 - 2 * core
    partners = [layer + bit * (1 - 2 * ((layer // bit) % 2)) for bit in (2 << k for k in range(stages))]
    barrier = pltpu.get_barrier_semaphore()
    for side in range(2):

        @pl.when(has[side])
        def _(side=side):
            pl.semaphore_signal(barrier, inc=1, device_id={"train": neighbour[side]}, device_id_type=MESH)

    pl.semaphore_signal(barrier, inc=1, device_id={"groups": other}, device_id_type=MESH)
    for partner in [sibling] + partners:
        pl.semaphore_signal(barrier, inc=1, device_id={"layer": partner}, device_id_type=MESH)
    pl.semaphore_wait(barrier, 2 + stages + has[0].astype(jnp.int32) + has[1].astype(jnp.int32))

    def place(index, side, chunk):
        return pl.ds(pl.multiple_of(index * block + side * share + chunk * rows, rows), rows)

    def along_z(side, index, distance, chunk, source):
        return pltpu.make_async_remote_copy(
            src_ref=source,
            dst_ref=gathered.at[place(index, group, chunk)],
            send_sem=z_send.at[side, distance, chunk],
            recv_sem=z_recv.at[side, distance, chunk],
            device_id={"train": neighbour[side]},
            device_id_type=MESH,
        )

    def along_y(side, index, which, distance, chunk):
        return pltpu.make_async_remote_copy(
            src_ref=gathered.at[place(index, which, chunk)],
            dst_ref=gathered.at[place(index, which, chunk)],
            send_sem=y_send.at[side, distance, chunk],
            recv_sem=y_recv.at[side, distance, chunk],
            device_id={"groups": other},
            device_id_type=MESH,
        )

    def part_of(part):
        return pl.ds(pl.multiple_of(part * width, width), width)

    def to_core(side, index, distance, part):
        return pltpu.make_async_remote_copy(
            src_ref=give.at[block_of(index), part_of(part)],
            dst_ref=taken.at[block_of(index), part_of(part)],
            send_sem=c_send.at[side, distance, part],
            recv_sem=c_recv.at[side, distance, part],
            device_id={"layer": sibling},
            device_id_type=MESH,
        )

    def along_x(stage, side, index, distance, part):
        return pltpu.make_async_remote_copy(
            src_ref=x_out.at[stage, block_of(index), part_of(part)],
            dst_ref=x_in.at[stage, block_of(index), part_of(part)],
            send_sem=x_send.at[stage, side, distance, part],
            recv_sem=x_recv.at[stage, side, distance, part],
            device_id={"layer": partners[stage]},
            device_id_type=MESH,
        )

    def own(chunk):
        return own_ref.at[pl.ds(pl.multiple_of(group * share + chunk * rows, rows), rows)]

    def first(chunk, _):
        for side in range(2):

            @pl.when(has[side])
            def _(side=side):
                along_z(side, position, 0, chunk, own(chunk)).start()

        return 0

    lax.fori_loop(0, chunks, first, 0)
    move.wait()
    load.wait()

    def at(side, distance):
        if side == 1:
            return position - distance, position - distance >= 0
        return position + distance, (position + distance < cycle) & (distance > 0)

    def absorb(side, index, distance, part):
        for stage in range(stages):
            along_x(stage, side, index, distance, part).wait_recv()
            sums = total[block_of(index), part_of(part)] + x_in[stage, block_of(index), part_of(part)].astype(jnp.float32)
            total[block_of(index), part_of(part)] = sums
            if stage + 1 < stages:
                x_out[stage + 1, block_of(index), part_of(part)] = sums.astype(jnp.bfloat16)
                along_x(stage + 1, side, index, distance, part).start()

    def turn(step, _):
        def slot(chunk, _):
            for side in range(2):
                index = position - 1 - step if side == 1 else position + 1 + step
                arrives = index >= 0 if side == 1 else index < cycle

                @pl.when(arrives)
                def _(side=side, index=index):
                    here = gathered.at[place(index, group, chunk)]
                    along_z(side, index, step, chunk, here).wait_recv()

                    @pl.when(has[side])
                    def _():
                        along_z(side, index, step + 1, chunk, here).start()

                    along_y(side, index, group, step, chunk).start()

            for side in range(2):
                index, there = at(side, step - 1)

                @pl.when((step > 0) & there & (chunk < parts))
                def _(side=side, index=index):
                    absorb(side, index, step - 1, chunk)

            mine = chunk // parts
            part = chunk - mine * parts
            columns = pl.ds(
                pl.multiple_of(((1 - core) * (1 - mine) + core * mine) * half + part * width, width), width
            )
            for side in range(2):
                index, there = at(side, step)

                @pl.when(there)
                def _(side=side, index=index):
                    @pl.when((chunk == 0) & (step > 0))
                    def _():
                        def landed(piece, _):
                            along_y(side, index, other, step - 1, piece).wait_recv()
                            return 0

                        lax.fori_loop(0, chunks, landed, 0)

                    product = lax.dot_general(
                        gathered[block_of(index), :],
                        train[columns, :],
                        (((1,), (1,)), ((), ())),
                        preferred_element_type=jnp.float32,
                    )

                    @pl.when(mine == 0)
                    def _():
                        give[block_of(index), part_of(part)] = product
                        to_core(side, index, step, part).start()

                    @pl.when(mine == 1)
                    def _():
                        to_core(side, index, step, part).wait_recv()
                        sums = product + taken[block_of(index), part_of(part)]
                        total[block_of(index), part_of(part)] = sums
                        x_out[0, block_of(index), part_of(part)] = sums.astype(jnp.bfloat16)
                        along_x(0, side, index, step, part).start()

            return 0

        return lax.fori_loop(0, chunks, slot, 0)

    lax.fori_loop(0, cycle, turn, 0)

    for side in range(2):
        index, there = at(side, cycle - 1)

        @pl.when(there)
        def _(side=side, index=index):
            def rest(part, _):
                absorb(side, index, cycle - 1, part)
                return 0

            lax.fori_loop(0, parts, rest, 0)

    count = out_ref.shape[0]
    lanes = pl.ds(pl.multiple_of(core * half, half), half)
    step_rows = 8

    def pick(owner, target):
        def eight(i, _):
            picked = [
                total[pl.ds(order_ref[owner * count + i * step_rows + k], 1), :] for k in range(step_rows)
            ]
            target[pl.ds(pl.multiple_of(i * step_rows, step_rows), step_rows), :] = jnp.concatenate(picked, axis=0)
            return 0

        lax.fori_loop(0, count // step_rows, eight, 0)

    pick(sibling, handed)
    last = pltpu.make_async_remote_copy(
        src_ref=handed,
        dst_ref=out_ref.at[:, lanes],
        send_sem=last_sem.at[0],
        recv_sem=last_sem.at[1],
        device_id={"layer": sibling},
        device_id_type=MESH,
    )
    last.start()
    pick(layer, out_ref.at[:, lanes])

    def sent(step, _):
        def piece(chunk, _):
            for side in range(2):
                index = position - step if side == 1 else position + step
                held = index >= 0 if side == 1 else index < cycle

                @pl.when(held & has[side])
                def _(side=side):
                    along_z(side, position, step, chunk, own(chunk)).wait_send()

                came = index - 1 >= 0 if side == 1 else index + 1 < cycle

                @pl.when(came)
                def _(side=side):
                    along_y(side, position, group, step, chunk).wait_send()

                _, there = at(side, step)

                @pl.when(there & (chunk < parts))
                def _(side=side):
                    to_core(side, position, step, chunk).wait_send()
                    for stage in range(stages):
                        along_x(stage, side, position, step, chunk).wait_send()

            return 0

        return lax.fori_loop(0, chunks, piece, 0)

    lax.fori_loop(0, cycle, sent, 0)
    last.wait()


def scores_of(conditioned, train_flat, query_order):
    cycle = lax.axis_size("train")
    layers = lax.axis_size("layer")
    stages = (layers // 2).bit_length() - 1
    block, depth = conditioned.shape
    slots = train_flat.shape[0]
    queries = cycle * block
    count = queries // layers
    chunks = min(4, block // 2 // 16)
    parts = chunks // 2
    dma = pltpu.SemaphoreType.DMA
    return pl.pallas_call(
        functools.partial(gather_and_score, cycle, chunks, stages),
        out_shape=jax.ShapeDtypeStruct((count, slots), jnp.float32),
        in_specs=[
            pl.BlockSpec(memory_space=pltpu.VMEM),
            pl.BlockSpec(memory_space=pl.ANY),
            pl.BlockSpec(memory_space=pltpu.SMEM),
        ],
        out_specs=pl.BlockSpec(memory_space=pltpu.VMEM),
        scratch_shapes=[
            pltpu.VMEM((queries, depth), jnp.bfloat16),
            pltpu.VMEM((slots, depth), jnp.bfloat16),
            pltpu.VMEM((queries, slots // 2), jnp.float32),
            pltpu.VMEM((queries, slots // 2), jnp.float32),
            pltpu.VMEM((queries, slots // 2), jnp.float32),
            pltpu.VMEM((stages, queries, slots // 2), jnp.bfloat16),
            pltpu.VMEM((stages, queries, slots // 2), jnp.bfloat16),
            pltpu.VMEM((count, slots // 2), jnp.float32),
            dma((2, cycle, chunks)),
            dma((2, cycle, chunks)),
            dma((2, cycle, chunks)),
            dma((2, cycle, chunks)),
            dma((2, cycle, parts)),
            dma((2, cycle, parts)),
            dma((stages, 2, cycle, parts)),
            dma((stages, 2, cycle, parts)),
            dma((2,)),
            dma((2,)),
        ],
        compiler_params=pltpu.CompilerParams(
            collective_id=0, has_side_effects=True, vmem_limit_bytes=50 * 1024 * 1024
        ),
        cost_estimate=pl.CostEstimate(
            flops=2 * queries * slots * depth, bytes_accessed=2 * slots * depth, transcendentals=0
        ),
    )(conditioned, train_flat, query_order)


def body(query_grads, train_grads, left_inverse, right_inverse, valid_rows, query_order):
    conditioned = precondition(query_grads, left_inverse, right_inverse).reshape(query_grads.shape[0], -1)
    scores = scores_of(conditioned, train_grads.reshape(train_grads.shape[0], -1), query_order)
    live = jnp.arange(scores.shape[1], dtype=jnp.int32) < valid_rows[0]
    return jnp.where(live[None, :], scores, 0.0)


def solution(mesh):
    return jax.shard_map(
        body,
        mesh=mesh,
        in_specs=(
            P("train", "layer", None),
            P(("groups", "train"), "layer", None),
            P("layer", None, None),
            P("layer", None, None),
            P(("groups", "train")),
            P(),
        ),
        out_specs=P("layer", ("groups", "train")),
        check_vma=False,
    )
```

```python
import functools

import jax
import jax.numpy as jnp
from jax import lax
from jax.experimental import pallas as pl
from jax.experimental.pallas import tpu as pltpu
from jax.sharding import PartitionSpec as P


def precondition(gradients, left_factor, right_factor):
    row_count = gradients.shape[0]
    layer_count = left_factor.shape[0]
    order_in = left_factor.shape[-1]
    order_out = right_factor.shape[-1]
    matrix = gradients.astype(jnp.float32).reshape(row_count, layer_count, order_in, order_out)
    matrix = jnp.einsum("lab,rlbc->rlac", left_factor, matrix, precision=lax.Precision.HIGH)
    matrix = jnp.einsum("rlac,lcd->rlad", matrix, right_factor, precision=lax.Precision.HIGH)
    return matrix.reshape(row_count, layer_count, order_in * order_out).astype(jnp.bfloat16)


MESH = pl.DeviceIdType.MESH


def gather_and_score(cycle, chunks, pieces, stages, own_ref, train_ref, order_ref, out_ref, gathered, train, give, taken, total, x_out, x_in, handed,
                     z_send, z_recv, y_send, y_recv, c_send, c_recv, x_send, x_recv, local_sem, last_sem):
    position = lax.axis_index("train")
    group = lax.axis_index("groups")
    layer = lax.axis_index("layer")
    core = layer % 2
    block = own_ref.shape[0]
    share = block // 2
    rows = share // chunks
    parts = pieces // 2
    width = train.shape[0] // pieces
    pace = chunks // pieces
    half = parts * width
    load = pltpu.make_async_copy(train_ref, train, local_sem.at[0])
    load.start()

    def block_of(index):
        return pl.ds(pl.multiple_of(index * block, block), block)

    move = pltpu.make_async_copy(own_ref, gathered.at[block_of(position)], local_sem.at[1])
    move.start()

    has = (position > 0, position < cycle - 1)
    neighbour = ((position + cycle - 1) % cycle, (position + 1) % cycle)
    other = 1 - group
    sibling = layer + 1 - 2 * core
    partners = [layer + bit * (1 - 2 * ((layer // bit) % 2)) for bit in (2 << k for k in range(stages))]
    barrier = pltpu.get_barrier_semaphore()
    for side in range(2):

        @pl.when(has[side])
        def _(side=side):
            pl.semaphore_signal(barrier, inc=1, device_id={"train": neighbour[side]}, device_id_type=MESH)

    pl.semaphore_signal(barrier, inc=1, device_id={"groups": other}, device_id_type=MESH)
    for partner in [sibling] + partners:
        pl.semaphore_signal(barrier, inc=1, device_id={"layer": partner}, device_id_type=MESH)
    pl.semaphore_wait(barrier, 2 + stages + has[0].astype(jnp.int32) + has[1].astype(jnp.int32))

    def place(index, side, chunk):
        return pl.ds(pl.multiple_of(index * block + side * share + chunk * rows, rows), rows)

    def along_z(side, index, distance, chunk, source):
        return pltpu.make_async_remote_copy(
            src_ref=source,
            dst_ref=gathered.at[place(index, group, chunk)],
            send_sem=z_send.at[side, distance, chunk],
            recv_sem=z_recv.at[side, distance, chunk],
            device_id={"train": neighbour[side]},
            device_id_type=MESH,
        )

    def along_y(side, index, which, distance, chunk):
        return pltpu.make_async_remote_copy(
            src_ref=gathered.at[place(index, which, chunk)],
            dst_ref=gathered.at[place(index, which, chunk)],
            send_sem=y_send.at[side, distance, chunk],
            recv_sem=y_recv.at[side, distance, chunk],
            device_id={"groups": other},
            device_id_type=MESH,
        )

    def part_of(part):
        return pl.ds(pl.multiple_of(part * width, width), width)

    def to_core(side, index, distance, part):
        return pltpu.make_async_remote_copy(
            src_ref=give.at[block_of(index), part_of(part)],
            dst_ref=taken.at[block_of(index), part_of(part)],
            send_sem=c_send.at[side, distance, part],
            recv_sem=c_recv.at[side, distance, part],
            device_id={"layer": sibling},
            device_id_type=MESH,
        )

    def along_x(stage, side, index, distance, part):
        return pltpu.make_async_remote_copy(
            src_ref=x_out.at[stage, block_of(index), part_of(part)],
            dst_ref=x_in.at[stage, block_of(index), part_of(part)],
            send_sem=x_send.at[stage, side, distance, part],
            recv_sem=x_recv.at[stage, side, distance, part],
            device_id={"layer": partners[stage]},
            device_id_type=MESH,
        )

    def own(chunk):
        return own_ref.at[pl.ds(pl.multiple_of(group * share + chunk * rows, rows), rows)]

    def first(chunk, _):
        for side in range(2):

            @pl.when(has[side])
            def _(side=side):
                along_z(side, position, 0, chunk, own(chunk)).start()

        return 0

    lax.fori_loop(0, chunks, first, 0)
    move.wait()
    load.wait()

    def at(side, distance):
        if side == 1:
            return position - distance, position - distance >= 0
        return position + distance, (position + distance < cycle) & (distance > 0)

    def absorb(side, index, distance, part):
        for stage in range(stages):
            along_x(stage, side, index, distance, part).wait_recv()
            sums = total[block_of(index), part_of(part)] + x_in[stage, block_of(index), part_of(part)].astype(jnp.float32)
            total[block_of(index), part_of(part)] = sums
            if stage + 1 < stages:
                x_out[stage + 1, block_of(index), part_of(part)] = sums.astype(jnp.bfloat16)
                along_x(stage + 1, side, index, distance, part).start()

    def turn(step, _):
        def slot(chunk, _):
            for side in range(2):
                index = position - 1 - step if side == 1 else position + 1 + step
                arrives = index >= 0 if side == 1 else index < cycle

                @pl.when(arrives)
                def _(side=side, index=index):
                    here = gathered.at[place(index, group, chunk)]
                    along_z(side, index, step, chunk, here).wait_recv()

                    @pl.when(has[side])
                    def _():
                        along_z(side, index, step + 1, chunk, here).start()

                    along_y(side, index, group, step, chunk).start()

            piece = chunk // pace
            due = chunk % pace == 0
            for side in range(2):
                index, there = at(side, step - 1)

                @pl.when((step > 0) & there & due & (piece < parts))
                def _(side=side, index=index):
                    absorb(side, index, step - 1, piece)

            mine = piece // parts
            part = piece - mine * parts
            columns = pl.ds(
                pl.multiple_of(((1 - core) * (1 - mine) + core * mine) * half + part * width, width), width
            )
            for side in range(2):
                index, there = at(side, step)

                @pl.when(there & due)
                def _(side=side, index=index):
                    @pl.when((chunk == 0) & (step > 0))
                    def _():
                        def landed(k, _):
                            along_y(side, index, other, step - 1, k).wait_recv()
                            return 0

                        lax.fori_loop(0, chunks, landed, 0)

                    product = lax.dot_general(
                        gathered[block_of(index), :],
                        train[columns, :],
                        (((1,), (1,)), ((), ())),
                        preferred_element_type=jnp.float32,
                    )

                    @pl.when(mine == 0)
                    def _():
                        give[block_of(index), part_of(part)] = product
                        to_core(side, index, step, part).start()

                    @pl.when(mine == 1)
                    def _():
                        to_core(side, index, step, part).wait_recv()
                        sums = product + taken[block_of(index), part_of(part)]
                        total[block_of(index), part_of(part)] = sums
                        x_out[0, block_of(index), part_of(part)] = sums.astype(jnp.bfloat16)
                        along_x(0, side, index, step, part).start()

            return 0

        return lax.fori_loop(0, chunks, slot, 0)

    lax.fori_loop(0, cycle, turn, 0)

    for side in range(2):
        index, there = at(side, cycle - 1)

        @pl.when(there)
        def _(side=side, index=index):
            def rest(part, _):
                absorb(side, index, cycle - 1, part)
                return 0

            lax.fori_loop(0, parts, rest, 0)

    count = out_ref.shape[0]
    lanes = pl.ds(pl.multiple_of(core * half, half), half)
    step_rows = 8

    def pick(owner, target):
        def eight(i, _):
            picked = [
                total[pl.ds(order_ref[owner * count + i * step_rows + k], 1), :] for k in range(step_rows)
            ]
            target[pl.ds(pl.multiple_of(i * step_rows, step_rows), step_rows), :] = jnp.concatenate(picked, axis=0)
            return 0

        lax.fori_loop(0, count // step_rows, eight, 0)

    pick(sibling, handed)
    last = pltpu.make_async_remote_copy(
        src_ref=handed,
        dst_ref=out_ref.at[:, lanes],
        send_sem=last_sem.at[0],
        recv_sem=last_sem.at[1],
        device_id={"layer": sibling},
        device_id_type=MESH,
    )
    last.start()
    pick(layer, out_ref.at[:, lanes])

    def sent(step, _):
        def piece(chunk, _):
            for side in range(2):
                index = position - step if side == 1 else position + step
                held = index >= 0 if side == 1 else index < cycle

                @pl.when(held & has[side])
                def _(side=side):
                    along_z(side, position, step, chunk, own(chunk)).wait_send()

                came = index - 1 >= 0 if side == 1 else index + 1 < cycle

                @pl.when(came)
                def _(side=side):
                    along_y(side, position, group, step, chunk).wait_send()

                _, there = at(side, step)

                @pl.when(there & (chunk < parts))
                def _(side=side):
                    to_core(side, position, step, chunk).wait_send()
                    for stage in range(stages):
                        along_x(stage, side, position, step, chunk).wait_send()

            return 0

        return lax.fori_loop(0, chunks, piece, 0)

    lax.fori_loop(0, cycle, sent, 0)
    last.wait()


def scores_of(conditioned, train_flat, query_order):
    cycle = lax.axis_size("train")
    layers = lax.axis_size("layer")
    stages = (layers // 2).bit_length() - 1
    block, depth = conditioned.shape
    slots = train_flat.shape[0]
    queries = cycle * block
    count = queries // layers
    chunks = min(8, block // 2 // 16)
    pieces = min(4, chunks)
    parts = pieces // 2
    dma = pltpu.SemaphoreType.DMA
    return pl.pallas_call(
        functools.partial(gather_and_score, cycle, chunks, pieces, stages),
        out_shape=jax.ShapeDtypeStruct((count, slots), jnp.float32),
        in_specs=[
            pl.BlockSpec(memory_space=pltpu.VMEM),
            pl.BlockSpec(memory_space=pl.ANY),
            pl.BlockSpec(memory_space=pltpu.SMEM),
        ],
        out_specs=pl.BlockSpec(memory_space=pltpu.VMEM),
        scratch_shapes=[
            pltpu.VMEM((queries, depth), jnp.bfloat16),
            pltpu.VMEM((slots, depth), jnp.bfloat16),
            pltpu.VMEM((queries, slots // 2), jnp.float32),
            pltpu.VMEM((queries, slots // 2), jnp.float32),
            pltpu.VMEM((queries, slots // 2), jnp.float32),
            pltpu.VMEM((stages, queries, slots // 2), jnp.bfloat16),
            pltpu.VMEM((stages, queries, slots // 2), jnp.bfloat16),
            pltpu.VMEM((count, slots // 2), jnp.float32),
            dma((2, cycle, chunks)),
            dma((2, cycle, chunks)),
            dma((2, cycle, chunks)),
            dma((2, cycle, chunks)),
            dma((2, cycle, parts)),
            dma((2, cycle, parts)),
            dma((stages, 2, cycle, parts)),
            dma((stages, 2, cycle, parts)),
            dma((2,)),
            dma((2,)),
        ],
        compiler_params=pltpu.CompilerParams(
            collective_id=0, has_side_effects=True, vmem_limit_bytes=50 * 1024 * 1024
        ),
        cost_estimate=pl.CostEstimate(
            flops=2 * queries * slots * depth, bytes_accessed=2 * slots * depth, transcendentals=0
        ),
    )(conditioned, train_flat, query_order)


def body(query_grads, train_grads, left_inverse, right_inverse, valid_rows, query_order):
    conditioned = precondition(query_grads, left_inverse, right_inverse).reshape(query_grads.shape[0], -1)
    scores = scores_of(conditioned, train_grads.reshape(train_grads.shape[0], -1), query_order)
    live = jnp.arange(scores.shape[1], dtype=jnp.int32) < valid_rows[0]
    return jnp.where(live[None, :], scores, 0.0)


def solution(mesh):
    return jax.shard_map(
        body,
        mesh=mesh,
        in_specs=(
            P("train", "layer", None),
            P(("groups", "train"), "layer", None),
            P("layer", None, None),
            P("layer", None, None),
            P(("groups", "train")),
            P(),
        ),
        out_specs=P("layer", ("groups", "train")),
        check_vma=False,
    )
```
